32 devices in a mesh: tm: 16 (over z, x, core), rows: 2 (over y).
Axes of the slice: x: 2, y: 2, z: 4, core: 2. Of those that a mesh axis runs over, the one named last changes fastest.
Arguments:
- video: bfloat16 [32, 4, 64, 384], P('tm', 'rows'), may hold values from -6 to 6
- conv_weight: bfloat16 [3, 3, 3, 384, 384], replicated, may hold values from -0.0625 to 0.0625
- norm_gain: float32 [384], replicated, may hold values from 0.1 to 1.9
- w_query: bfloat16 [384, 384], replicated, may hold values from -0.3125 to 0.3125
- w_key: bfloat16 [384, 384], replicated, may hold values from -0.875 to 0.875
- w_value: bfloat16 [384, 384], replicated, may hold values from -0.875 to 0.875
- w_out: bfloat16 [384, 384], replicated, may hold values from -0.3125 to 0.3125
- cotangent: bfloat16 [32, 4, 64, 384], P('tm', 'rows'), may hold values from -6 to 6
Outputs:
- block_out: bfloat16 [32, 4, 64, 384], P('tm', 'rows')
- video_grad: bfloat16 [32, 4, 64, 384], P('tm', 'rows')
The draws below stay inside these ranges and needn't reach their ends.
All inputs are finite; a program needn't handle non-finite values.
Results may differ from the reference program's by a relative error of at most 0.014.
Values may be sent and summed in bfloat16 or wider, within the bound.
A program may use at most 64 MiB of HBM per device.

```python
import jax
import jax.numpy as jnp
from jax import lax

CHANNELS = 384
WIDTH = 64
FRAMES = 32
HEIGHT = 4


def block_scale(key, extent, split, smallest, top_value):
    def one(axis_at, shards_of):
        steps = jax.random.uniform(jax.random.fold_in(jax.random.fold_in(key, 6), axis_at), (shards_of,), jnp.float32, smallest / len(split), top_value / len(split))
        return jnp.repeat(jnp.exp(steps), extent[axis_at] // shards_of).reshape((-1,) + (1,) * (len(extent) - axis_at - 1))

    factor_of = one(*split[0])
    for cut in split[1:]:
        factor_of = factor_of * one(*cut)
    return factor_of


def noise(key, dims, scale, most, shards=(), held_as=jnp.bfloat16):
    entries = scale * jax.random.normal(key, dims, jnp.float32)
    if shards:
        entries = entries * block_scale(key, dims, shards, -0.22, 0.18)
    return jnp.clip(entries, -most, most).astype(held_as)


def setup_inputs(seed: int = 0) -> dict:
    splits = jax.random.split(jax.random.key(seed), 9)
    return {
        "video": noise(splits[0], (FRAMES, HEIGHT, WIDTH, CHANNELS), 1.0, 6.0, ((0, 16), (1, 2))),
        "conv_weight": noise(splits[1], (3, 3, 3, CHANNELS, CHANNELS), (27 * CHANNELS) ** -0.5, 0.0625),
        "norm_gain": jnp.clip(1.0 + 0.18 * jax.random.normal(splits[2], (CHANNELS,), jnp.float32), 0.1, 1.9),
        "w_query": noise(splits[3], (CHANNELS, CHANNELS), CHANNELS ** -0.5, 0.3125),
        "w_key": noise(splits[4], (CHANNELS, CHANNELS), (CHANNELS // 8) ** -0.5, 0.875),
        "w_value": noise(splits[5], (CHANNELS, CHANNELS), (CHANNELS // 8) ** -0.5, 0.875),
        "w_out": noise(splits[6], (CHANNELS, CHANNELS), CHANNELS ** -0.5, 0.3125),
        "cotangent": noise(splits[7], (FRAMES, HEIGHT, WIDTH, CHANNELS), 1.0, 6.0, ((0, 16), (1, 2))),
    }


def convolve(padded, kernel, pads):
    result = lax.conv_general_dilated(padded[None], kernel, (1, 1, 1), pads, dimension_numbers=('NDHWC', 'DHWIO', 'NDHWC'), preferred_element_type=jnp.float32)
    return result[0]

def reference(video, conv_weight, norm_gain, w_query, w_key, w_value, w_out, cotangent):
    chans = video.shape[3]
    scale = 1.0 / jnp.sqrt(jnp.float32(chans))
    padded = jnp.pad(video, ((2, 0), (1, 1), (1, 1), (0, 0)))
    conv = convolve(padded, conv_weight, [(0, 0), (0, 0), (0, 0)]).astype(jnp.bfloat16)
    convf = conv.astype(jnp.float32)
    inverse = lax.rsqrt(lax.optimization_barrier(jnp.mean(convf * convf, axis=-1, keepdims=True)) + 1e-06)
    normed = convf * inverse * norm_gain
    act = jax.nn.silu(normed).astype(jnp.bfloat16)
    frames = video.shape[0]
    flat = act.reshape(-1, chans)
    queries = jnp.dot(flat, w_query, preferred_element_type=jnp.float32).astype(jnp.bfloat16).reshape(frames, -1, chans)
    keys = jnp.dot(flat, w_key, preferred_element_type=jnp.float32).astype(jnp.bfloat16).reshape(frames, -1, chans)
    values = jnp.dot(flat, w_value, preferred_element_type=jnp.float32).astype(jnp.bfloat16).reshape(frames, -1, chans)

    def forward_frame(items):
        query_f, key_f, value_f = items
        scores = jnp.dot(query_f, key_f.T, preferred_element_type=jnp.float32) * scale
        top = lax.optimization_barrier(jnp.max(scores, axis=-1, keepdims=True))
        expo = jnp.exp(scores - top)
        total = lax.optimization_barrier(jnp.sum(expo, axis=-1, keepdims=True))
        probs = expo / total
        attended = jnp.dot(probs.astype(jnp.bfloat16), value_f, preferred_element_type=jnp.float32).astype(jnp.bfloat16)
        return (attended, (top + jnp.log(total))[:, 0])
    attended, logsum = lax.map(forward_frame, (queries, keys, values))
    projected = jnp.dot(attended.reshape(-1, chans), w_out, preferred_element_type=jnp.float32)
    block_out = (act.astype(jnp.float32).reshape(-1, chans) + projected).astype(jnp.bfloat16).reshape(video.shape)
    grad_att = jnp.dot(cotangent.reshape(-1, chans), w_out.T, preferred_element_type=jnp.float32).astype(jnp.bfloat16).reshape(frames, -1, chans)

    def backward_frame(items):
        query_f, key_f, value_f, attended_f, grad_f, logsum_f = items
        scores = jnp.dot(query_f, key_f.T, preferred_element_type=jnp.float32) * scale
        probs = jnp.exp(scores - logsum_f[:, None])
        delta = lax.optimization_barrier(jnp.sum(grad_f.astype(jnp.float32) * attended_f.astype(jnp.float32), axis=-1))
        dprob = jnp.dot(grad_f, value_f.T, preferred_element_type=jnp.float32)
        dscore = (probs * (dprob - delta[:, None])).astype(jnp.bfloat16)
        grad_q = (jnp.dot(dscore, key_f, preferred_element_type=jnp.float32) * scale).astype(jnp.bfloat16)
        grad_k = (jnp.dot(dscore.T, query_f, preferred_element_type=jnp.float32) * scale).astype(jnp.bfloat16)
        grad_v = jnp.dot(probs.astype(jnp.bfloat16).T, grad_f, preferred_element_type=jnp.float32).astype(jnp.bfloat16)
        return (grad_q, grad_k, grad_v)
    grad_q, grad_k, grad_v = lax.map(backward_frame, (queries, keys, values, attended, grad_att, logsum))
    grad_act = cotangent.astype(jnp.float32).reshape(-1, chans)
    grad_act = grad_act + jnp.dot(grad_q.reshape(-1, chans), w_query.T, preferred_element_type=jnp.float32)
    grad_act = grad_act + jnp.dot(grad_k.reshape(-1, chans), w_key.T, preferred_element_type=jnp.float32)
    grad_act = grad_act + jnp.dot(grad_v.reshape(-1, chans), w_value.T, preferred_element_type=jnp.float32)
    grad_act = grad_act.reshape(video.shape)
    sigma = jax.nn.sigmoid(normed)
    grad_normed = grad_act * sigma * (1.0 + normed * (1.0 - sigma))
    scaled = grad_normed * norm_gain
    grad_conv = inverse * (scaled - convf * inverse * inverse * lax.optimization_barrier(jnp.mean(scaled * convf, axis=-1, keepdims=True)))
    grad_conv = grad_conv.astype(jnp.bfloat16)
    flipped = jnp.transpose(jnp.flip(conv_weight, (0, 1, 2)), (0, 1, 2, 4, 3))
    grad_padded = convolve(grad_conv, flipped, [(2, 2), (2, 2), (1, 1)])
    video_grad = grad_padded[2:, 1:-1].astype(jnp.bfloat16)
    return (block_out, video_grad)
```

```python
import functools

import jax
import jax.numpy as jnp
from jax import lax
from jax.experimental import pallas as pl
from jax.experimental.pallas import tpu as pltpu
from jax.sharding import PartitionSpec as P

TAPS = 3
BF = jnp.bfloat16
F32 = jnp.float32


def mm(a, b):
    return lax.dot_general(a, b, (((1,), (0,)), ((), ())), preferred_element_type=F32)


def mm_nt(a, b):
    return lax.dot_general(a, b, (((1,), (1,)), ((), ())), preferred_element_type=F32)


def mm_tn(a, b):
    return lax.dot_general(a, b, (((0,), (0,)), ((), ())), preferred_element_type=F32)


def block(
    n_tm,
    n_rows,
    video,
    weight,
    gain,
    w_query,
    w_key,
    w_value,
    w_out,
    cot,
    block_out,
    video_grad,
    xin,
    wbuf,
    wqkv,
    wo,
    cot_full,
    conv_full,
    sums,
    act_s,
    att_s,
    gc_full,
    gwin,
    w_sem,
    p_sem,
    io_sem,
    halo_send,
    halo_recv,
    cot_send,
    cot_recv,
    conv_send,
    conv_recv,
    gc_send,
    gc_recv,
):
    frames, h, width, chans = video.shape
    full = n_rows * h
    pos = full * width
    own = frames * h * width
    tm = lax.axis_index("tm")
    row = lax.axis_index("rows")
    scale = 1.0 / jnp.sqrt(jnp.float32(chans))
    first_row, last_row = row == 0, row == n_rows - 1
    has_up, has_down = row > 0, row < n_rows - 1
    has_prev, has_next = tm > 0, tm < n_tm - 1
    own_rows = pl.ds(row * h, h)

    w_copies = {
        (a, b): pltpu.make_async_copy(weight.at[a, b], wbuf.at[a, b], w_sem.at[a, b])
        for a in range(TAPS)
        for b in range(TAPS)
    }
    in_copy = pltpu.make_async_copy(video, xin.at[pl.ds(2, frames), pl.ds(1, h)], io_sem.at[0])
    cot_copy = pltpu.make_async_copy(cot, cot_full.at[:, own_rows], io_sem.at[1])
    p_copies = [
        pltpu.make_async_copy(w, wqkv.at[:, pl.ds(i * chans, chans)], p_sem.at[i])
        for i, w in enumerate((w_query, w_key, w_value))
    ] + [pltpu.make_async_copy(w_out, wo, p_sem.at[3])]

    in_copy.start()
    for a in (2, 1, 0):
        for b in range(TAPS):
            w_copies[a, b].start()
    cot_copy.start()
    for c in p_copies:
        c.start()

    barrier = pltpu.get_barrier_semaphore()

    def greet(cond, t, r):
        @pl.when(cond)
        def _():
            pl.semaphore_signal(
                barrier, inc=1, device_id=(t, r), device_id_type=pl.DeviceIdType.MESH
            )

    peers = [lax.rem(row + k, n_rows) for k in range(1, n_rows)]
    for peer in peers:
        pl.semaphore_signal(
            barrier, inc=1, device_id=(tm, peer), device_id_type=pl.DeviceIdType.MESH
        )
    greet(has_prev, tm - 1, row)
    greet(has_prev & has_up, tm - 1, row - 1)
    greet(has_prev & has_down, tm - 1, row + 1)
    greet(has_next, tm + 1, row)

    line = jnp.zeros((frames, width, chans), BF)

    @pl.when(first_row)
    def _():
        xin[2 : 2 + frames, 0] = line
        xin[0:2, 0] = jnp.zeros((2, width, chans), BF)

    @pl.when(last_row)
    def _():
        xin[2 : 2 + frames, h + 1] = line
        xin[0:2, h + 1] = jnp.zeros((2, width, chans), BF)

    @pl.when(tm == 0)
    def _():
        xin[0:2] = jnp.zeros((2, h + 2, width, chans), BF)

    @pl.when(tm == n_tm - 1)
    def _():
        gwin[frames : frames + 2] = jnp.zeros((2, h + 2, width, chans), BF)

    gc_full[0] = jnp.zeros((width, chans), BF)
    gc_full[full + 1] = jnp.zeros((width, chans), BF)

    wait_for = (
        (n_rows - 1)
        + jnp.where(has_prev, 1, 0)
        + jnp.where(has_next, 1 + jnp.where(has_up, 1, 0) + jnp.where(has_down, 1, 0), 0)
    )
    pl.semaphore_wait(barrier, wait_for)

    def remote(src, dst, send, recv, t, r):
        return pltpu.make_async_remote_copy(
            src_ref=src,
            dst_ref=dst,
            send_sem=send,
            recv_sem=recv,
            device_id=(t, r),
            device_id_type=pl.DeviceIdType.MESH,
        )

    now, before = pl.ds(2, frames), pl.ds(0, 2)
    late = pl.ds(frames - 2, 2)
    top, low = pl.ds(0, 1), pl.ds(h - 1, 1)
    halos = [
        (has_up, remote(video.at[:, top], xin.at[now, pl.ds(h + 1, 1)], halo_send.at[0], halo_recv.at[0], tm, row - 1), has_down),
        (has_down, remote(video.at[:, low], xin.at[now, pl.ds(0, 1)], halo_send.at[1], halo_recv.at[1], tm, row + 1), has_up),
        (has_next & has_up, remote(video.at[late, top], xin.at[before, pl.ds(h + 1, 1)], halo_send.at[2], halo_recv.at[2], tm + 1, row - 1), has_prev & has_down),
        (has_next & has_down, remote(video.at[late, low], xin.at[before, pl.ds(0, 1)], halo_send.at[3], halo_recv.at[3], tm + 1, row + 1), has_prev & has_up),
        (has_next, remote(video.at[late], xin.at[before, pl.ds(1, h)], halo_send.at[4], halo_recv.at[4], tm + 1, row), has_prev),
    ]
    for cond, copy, _ in halos:
        pl.when(cond)(copy.start)

    def conv_step(a):
        lhs = jnp.concatenate(
            [xin[a : a + frames, b : b + h].reshape(own, chans) for b in range(TAPS)], axis=1
        )
        rhs = jnp.concatenate(
            [wbuf[a, :, c].reshape(TAPS * chans, chans) for c in range(TAPS)], axis=1
        )
        return mm(lhs, rhs)

    column = lax.rem(lax.broadcasted_iota(jnp.int32, (own, 1), 0), width)

    def shifted(x, by):
        rolled = pltpu.roll(x, by % own, 0)
        edge = column == (0 if by == 1 else width - 1)
        return jnp.where(edge, 0.0, rolled)

    def part(c):
        return sums[:, c * chans : (c + 1) * chans]

    in_copy.wait()
    for _, copy, cond in halos[:2]:
        pl.when(cond)(copy.wait_recv)
    for b in range(TAPS):
        w_copies[2, b].wait()
    sums[...] = conv_step(2)
    cots = [
        remote(cot, cot_full.at[:, own_rows], cot_send.at[k], cot_recv.at[k], tm, peer)
        for k, peer in enumerate(peers)
    ]
    for copy in cots:
        copy.start()
    for _, copy, cond in halos[2:]:
        pl.when(cond)(copy.wait_recv)
    for a in (1, 0):
        for b in range(TAPS):
            w_copies[a, b].wait()
        sums[...] += conv_step(a)
    conv = (shifted(part(0), 1) + part(1) + shifted(part(2), -1)).astype(BF)
    conv_full[:, own_rows] = conv.reshape(frames, h, width, chans)
    convs = [
        remote(
            conv_full.at[:, own_rows],
            conv_full.at[:, own_rows],
            conv_send.at[k],
            conv_recv.at[k],
            tm,
            peer,
        )
        for k, peer in enumerate(peers)
    ]
    for copy in convs:
        copy.start()
    for c in p_copies:
        c.wait()
    cot_copy.wait()
    for copy in cots:
        copy.wait_recv()
    for copy in convs:
        copy.wait_recv()

    g = gain[...]
    mine = pl.ds(pl.multiple_of(row * (h * width), h * width), h * width)
    backs = []
    for f in range(frames):
        convf = conv_full[f].reshape(pos, chans).astype(F32)
        inverse = lax.rsqrt(jnp.mean(convf * convf, axis=-1, keepdims=True) + 1e-06)
        normed = convf * inverse * g
        sigma = 1.0 / (1.0 + jnp.exp(-normed))
        act = (normed * sigma).astype(BF)
        act_s[...] = act
        qkv = mm(act, wqkv[...]).astype(BF)
        query = qkv[:, :chans]
        key = qkv[:, chans : 2 * chans]
        value = qkv[:, 2 * chans :]
        cot_f = cot_full[f].reshape(pos, chans)
        grad_att = mm_nt(cot_f, wo[...]).astype(BF)
        scores = mm_nt(query, key) * scale
        peak = jnp.max(scores, axis=-1, keepdims=True)
        expo = jnp.exp(scores - peak)
        probs = expo / jnp.sum(expo, axis=-1, keepdims=True)
        probs_b = probs.astype(BF)
        attended = mm(probs_b, value).astype(BF)
        att_s[...] = attended
        delta = jnp.sum(grad_att.astype(F32) * attended.astype(F32), axis=-1, keepdims=True)
        dprob = mm_nt(grad_att, value)
        dscore = (probs * (dprob - delta)).astype(BF)
        grad_q = (mm(dscore, key) * scale).astype(BF)
        grad_k = (mm_tn(dscore, query) * scale).astype(BF)
        grad_v = mm_tn(probs_b, grad_att).astype(BF)
        grads = jnp.concatenate([grad_q, grad_k, grad_v], axis=1)
        grad_act = cot_f.astype(F32) + mm_nt(grads, wqkv[...])
        scaled = grad_act * sigma * (1.0 + normed * (1.0 - sigma)) * g
        grad_conv = inverse * (
            scaled
            - convf * inverse * inverse * jnp.mean(scaled * convf, axis=-1, keepdims=True)
        )
        gc_full[1 : full + 1] = grad_conv.astype(BF).reshape(full, width, chans)
        gwin[f] = gc_full[pl.ds(row * h, h + 2)]
        if f < 2:
            back = remote(
                gwin.at[f], gwin.at[frames + f], gc_send.at[f], gc_recv.at[f], tm - 1, row
            )
            pl.when(has_prev)(back.start)
            backs.append(back)
        projected = mm(att_s[mine], wo[...])
        out = (act_s[mine].astype(F32) + projected).astype(BF)
        block_out[f] = out.reshape(h, width, chans)

    def back_step(a):
        lhs = jnp.concatenate(
            [
                gwin[2 - a : 2 - a + frames, 2 - b : 2 - b + h].reshape(own, chans)
                for b in range(TAPS)
            ],
            axis=1,
        )
        rhs = jnp.concatenate(
            [wbuf[a, b].reshape(TAPS * chans, chans) for b in range(TAPS)], axis=1
        )
        return mm_nt(lhs, rhs)

    sums[...] = back_step(2)
    for back in backs:
        pl.when(has_next)(back.wait_recv)
    sums[...] += back_step(1)
    sums[...] += back_step(0)
    result = shifted(part(0), -1) + part(1) + shifted(part(2), 1)
    video_grad[...] = result.astype(BF).reshape(frames, h, width, chans)

    for cond, copy, _ in halos:
        pl.when(cond)(copy.wait_send)
    for copy in cots + convs:
        copy.wait_send()
    for back in backs:
        pl.when(has_prev)(back.wait_send)


def local(n_tm, n_rows, video, conv_weight, norm_gain, w_query, w_key, w_value, w_out, cotangent):
    frames, h, width, chans = video.shape
    full = n_rows * h
    own = frames * h * width
    anywhere = pl.BlockSpec(memory_space=pl.ANY)
    vmem = pl.BlockSpec(memory_space=pltpu.VMEM)
    dma = pltpu.SemaphoreType.DMA
    shape = jax.ShapeDtypeStruct(video.shape, BF)
    return pl.pallas_call(
        functools.partial(block, n_tm, n_rows),
        out_shape=(shape, shape),
        in_specs=[anywhere, anywhere, vmem] + [anywhere] * 5,
        out_specs=(vmem, vmem),
        scratch_shapes=[
            pltpu.VMEM((frames + 2, h + 2, width, chans), BF),
            pltpu.VMEM(conv_weight.shape, BF),
            pltpu.VMEM((chans, 3 * chans), BF),
            pltpu.VMEM((chans, chans), BF),
            pltpu.VMEM((frames, full, width, chans), BF),
            pltpu.VMEM((frames, full, width, chans), BF),
            pltpu.VMEM((own, TAPS * chans), F32),
            pltpu.VMEM((full * width, chans), BF),
            pltpu.VMEM((full * width, chans), BF),
            pltpu.VMEM((full + 2, width, chans), BF),
            pltpu.VMEM((frames + 2, h + 2, width, chans), BF),
            dma((TAPS, TAPS)),
            dma((4,)),
            dma((2,)),
            dma((5,)),
            dma((5,)),
            dma((n_rows - 1,)),
            dma((n_rows - 1,)),
            dma((n_rows - 1,)),
            dma((n_rows - 1,)),
            dma((2,)),
            dma((2,)),
        ],
        compiler_params=pltpu.CompilerParams(
            collective_id=0, has_side_effects=True, vmem_limit_bytes=56 * 1024 * 1024
        ),
    )(
        video,
        conv_weight,
        norm_gain.reshape(1, chans),
        w_query,
        w_key,
        w_value,
        w_out,
        cotangent,
    )


def solution(mesh):
    n_tm, n_rows = mesh.shape["tm"], mesh.shape["rows"]
    split = P("tm", "rows", None, None)
    return jax.shard_map(
        functools.partial(local, n_tm, n_rows),
        mesh=mesh,
        in_specs=(split, P(), P(), P(), P(), P(), P(), split),
        out_specs=(split, split),
        check_vma=False,
    )
```

```python
import functools

import jax
import jax.numpy as jnp
from jax import lax
from jax.experimental import pallas as pl
from jax.experimental.pallas import tpu as pltpu
from jax.sharding import PartitionSpec as P

TAPS = 3
BF = jnp.bfloat16
F32 = jnp.float32


def mm(a, b):
    return lax.dot_general(a, b, (((1,), (0,)), ((), ())), preferred_element_type=F32)


def mm_nt(a, b):
    return lax.dot_general(a, b, (((1,), (1,)), ((), ())), preferred_element_type=F32)


def mm_tn(a, b):
    return lax.dot_general(a, b, (((0,), (0,)), ((), ())), preferred_element_type=F32)


def block(
    n_tm,
    n_rows,
    video,
    weight,
    gain,
    w_query,
    w_key,
    w_value,
    w_out,
    cot,
    block_out,
    video_grad,
    xin,
    wbuf,
    wqkv,
    wo,
    cot_full,
    conv_full,
    sums,
    act_s,
    att_s,
    gc_full,
    grad_s,
    gwin,
    w_sem,
    p_sem,
    io_sem,
    halo_send,
    halo_recv,
    cot_send,
    cot_recv,
    conv_send,
    conv_recv,
    gc_send,
    gc_recv,
):
    frames, h, width, chans = video.shape
    full = n_rows * h
    pos = full * width
    own = frames * h * width
    tm = lax.axis_index("tm")
    row = lax.axis_index("rows")
    scale = 1.0 / jnp.sqrt(jnp.float32(chans))
    first_row, last_row = row == 0, row == n_rows - 1
    has_up, has_down = row > 0, row < n_rows - 1
    has_prev, has_next = tm > 0, tm < n_tm - 1
    own_rows = pl.ds(row * h, h)

    w_copies = {
        (a, b): pltpu.make_async_copy(weight.at[a, b], wbuf.at[a, b], w_sem.at[a, b])
        for a in range(TAPS)
        for b in range(TAPS)
    }
    in_copy = pltpu.make_async_copy(video, xin.at[pl.ds(2, frames), pl.ds(1, h)], io_sem.at[0])
    cot_copy = pltpu.make_async_copy(cot, cot_full.at[:, own_rows], io_sem.at[1])
    p_copies = [
        pltpu.make_async_copy(w, wqkv.at[:, pl.ds(i * chans, chans)], p_sem.at[i])
        for i, w in enumerate((w_query, w_key, w_value))
    ] + [pltpu.make_async_copy(w_out, wo, p_sem.at[3])]

    in_copy.start()
    for a in (2, 1, 0):
        for b in range(TAPS):
            w_copies[a, b].start()
    cot_copy.start()
    for c in p_copies:
        c.start()

    barrier = pltpu.get_barrier_semaphore()

    def greet(cond, t, r):
        @pl.when(cond)
        def _():
            pl.semaphore_signal(
                barrier, inc=1, device_id=(t, r), device_id_type=pl.DeviceIdType.MESH
            )

    peers = [lax.rem(row + k, n_rows) for k in range(1, n_rows)]
    for peer in peers:
        pl.semaphore_signal(
            barrier, inc=1, device_id=(tm, peer), device_id_type=pl.DeviceIdType.MESH
        )
    greet(has_prev, tm - 1, row)
    greet(has_next, tm + 1, row)

    line = jnp.zeros((frames, width, chans), BF)

    @pl.when(first_row)
    def _():
        xin[2 : 2 + frames, 0] = line
        xin[0:2, 0] = jnp.zeros((2, width, chans), BF)

    @pl.when(last_row)
    def _():
        xin[2 : 2 + frames, h + 1] = line
        xin[0:2, h + 1] = jnp.zeros((2, width, chans), BF)

    @pl.when(tm == 0)
    def _():
        xin[0:2] = jnp.zeros((2, h + 2, width, chans), BF)

    @pl.when(tm == n_tm - 1)
    def _():
        gwin[frames : frames + 2] = jnp.zeros((2, h + 2, width, chans), BF)

    gc_full[0] = jnp.zeros((width, chans), BF)
    gc_full[full + 1] = jnp.zeros((width, chans), BF)

    wait_for = (
        (n_rows - 1)
        + jnp.where(has_prev, 1, 0)
        + jnp.where(has_next, 1, 0)
    )
    pl.semaphore_wait(barrier, wait_for)

    def remote(src, dst, send, recv, t, r):
        return pltpu.make_async_remote_copy(
            src_ref=src,
            dst_ref=dst,
            send_sem=send,
            recv_sem=recv,
            device_id=(t, r),
            device_id_type=pl.DeviceIdType.MESH,
        )

    now, before = pl.ds(2, frames), pl.ds(0, 2)
    late = pl.ds(frames - 2, 2)
    top, low = pl.ds(0, 1), pl.ds(h - 1, 1)
    halos = [
        (has_up, remote(video.at[:, top], xin.at[now, pl.ds(h + 1, 1)], halo_send.at[0], halo_recv.at[0], tm, row - 1), has_down),
        (has_down, remote(video.at[:, low], xin.at[now, pl.ds(0, 1)], halo_send.at[1], halo_recv.at[1], tm, row + 1), has_up),
        (has_next, remote(video.at[late], xin.at[before, pl.ds(1, h)], halo_send.at[2], halo_recv.at[2], tm + 1, row), has_prev),
    ]
    last = pl.ds(frames, 2)
    edges = [
        (cond, pl.ds(i, 1), halo_send.at[k], halo_recv.at[k])
        for cond, i, k in ((has_up, 0, 3), (has_down, h + 1, 4))
    ]
    passed = [
        (has_next & cond, remote(xin.at[last, i], xin.at[before, i], ss, rs, tm + 1, row), has_prev & cond)
        for cond, i, ss, rs in edges
    ]
    for cond, copy, _ in halos:
        pl.when(cond)(copy.start)

    def conv_step(a):
        lhs = jnp.concatenate(
            [xin[a : a + frames, b : b + h].reshape(own, chans) for b in range(TAPS)], axis=1
        )
        rhs = jnp.concatenate(
            [wbuf[a, :, c].reshape(TAPS * chans, chans) for c in range(TAPS)], axis=1
        )
        return mm(lhs, rhs)

    column = lax.rem(lax.broadcasted_iota(jnp.int32, (own, 1), 0), width)

    def shifted(x, by):
        rolled = pltpu.roll(x, by % own, 0)
        edge = column == (0 if by == 1 else width - 1)
        return jnp.where(edge, 0.0, rolled)

    def part(c):
        return sums[:, c * chans : (c + 1) * chans]

    in_copy.wait()
    for _, copy, cond in halos[:2]:
        pl.when(cond)(copy.wait_recv)
    for cond, copy, _ in passed:
        pl.when(cond)(copy.start)
    cots = [
        remote(
            cot.at[f], cot_full.at[f, own_rows], cot_send.at[f, k], cot_recv.at[f, k], tm, peer
        )
        for f in range(frames)
        for k, peer in enumerate(peers)
    ]
    for copy in cots:
        copy.start()
    for b in range(TAPS):
        w_copies[2, b].wait()
    sums[...] = conv_step(2)
    for _, copy, cond in halos[2:] + passed:
        pl.when(cond)(copy.wait_recv)
    for a in (1, 0):
        for b in range(TAPS):
            w_copies[a, b].wait()
        sums[...] += conv_step(a)
    conv = (shifted(part(0), 1) + part(1) + shifted(part(2), -1)).astype(BF)
    conv_full[:, own_rows] = conv.reshape(frames, h, width, chans)
    convs = [
        [
            remote(
                conv_full.at[f, own_rows],
                conv_full.at[f, own_rows],
                conv_send.at[f, k],
                conv_recv.at[f, k],
                tm,
                peer,
            )
            for k, peer in enumerate(peers)
        ]
        for f in range(frames)
    ]
    for group in convs:
        for copy in group:
            copy.start()
    for c in p_copies:
        c.wait()
    cot_copy.wait()
    for copy in cots:
        copy.wait_recv()
    for f in range(frames):
        grad_s[f] = mm_nt(cot_full[f].reshape(pos, chans), wo[...]).astype(BF)

    g = gain[...].reshape(1, chans)
    mine = pl.ds(pl.multiple_of(row * (h * width), h * width), h * width)
    backs = []
    for f in range(frames):
        for copy in convs[f]:
            copy.wait_recv()
        convf = conv_full[f].reshape(pos, chans).astype(F32)
        inverse = lax.rsqrt(jnp.mean(convf * convf, axis=-1, keepdims=True) + 1e-06)
        normed = convf * inverse * g
        sigma = 1.0 / (1.0 + jnp.exp(-normed))
        act = (normed * sigma).astype(BF)
        act_s[...] = act
        qkv = mm(act, wqkv[...]).astype(BF)
        query = qkv[:, :chans]
        key = qkv[:, chans : 2 * chans]
        value = qkv[:, 2 * chans :]
        cot_f = cot_full[f].reshape(pos, chans)
        grad_att = grad_s[f]
        scores = mm_nt(query, key) * scale
        peak = jnp.max(scores, axis=-1, keepdims=True)
        expo = jnp.exp(scores - peak)
        probs = expo / jnp.sum(expo, axis=-1, keepdims=True)
        probs_b = probs.astype(BF)
        attended = mm(probs_b, value).astype(BF)
        att_s[...] = attended
        delta = jnp.sum(grad_att.astype(F32) * attended.astype(F32), axis=-1, keepdims=True)
        dprob = mm_nt(grad_att, value)
        dscore = (probs * (dprob - delta)).astype(BF)
        grad_q = (mm(dscore, key) * scale).astype(BF)
        grad_k = (mm_tn(dscore, query) * scale).astype(BF)
        grad_v = mm_tn(probs_b, grad_att).astype(BF)
        grads = jnp.concatenate([grad_q, grad_k, grad_v], axis=1)
        grad_act = cot_f.astype(F32) + mm_nt(grads, wqkv[...])
        scaled = grad_act * sigma * (1.0 + normed * (1.0 - sigma)) * g
        grad_conv = inverse * (
            scaled
            - convf * inverse * inverse * jnp.mean(scaled * convf, axis=-1, keepdims=True)
        )
        gc_full[1 : full + 1] = grad_conv.astype(BF).reshape(full, width, chans)
        gwin[f] = gc_full[pl.ds(row * h, h + 2)]
        if f < 2:
            back = remote(
                gwin.at[f], gwin.at[frames + f], gc_send.at[f], gc_recv.at[f], tm - 1, row
            )
            pl.when(has_prev)(back.start)
            backs.append(back)
        projected = mm(att_s[mine], wo[...])
        out = (act_s[mine].astype(F32) + projected).astype(BF)
        block_out[f] = out.reshape(h, width, chans)

    def back_step(a):
        lhs = jnp.concatenate(
            [
                gwin[2 - a : 2 - a + frames, 2 - b : 2 - b + h].reshape(own, chans)
                for b in range(TAPS)
            ],
            axis=1,
        )
        rhs = jnp.concatenate(
            [wbuf[a, b].reshape(TAPS * chans, chans) for b in range(TAPS)], axis=1
        )
        return mm_nt(lhs, rhs)

    sums[...] = back_step(2)
    pl.when(has_next)(backs[0].wait_recv)
    sums[...] += back_step(1)
    pl.when(has_next)(backs[1].wait_recv)
    sums[...] += back_step(0)
    result = shifted(part(0), -1) + part(1) + shifted(part(2), 1)
    video_grad[...] = result.astype(BF).reshape(frames, h, width, chans)

    for cond, copy, _ in halos + passed:
        pl.when(cond)(copy.wait_send)
    for copy in sum(convs, cots):
        copy.wait_send()
    for back in backs:
        pl.when(has_prev)(back.wait_send)


def settle(a, b, a_out, b_out):
    a_out[...] = a[...]
    b_out[...] = b[...]


def local(n_tm, n_rows, video, conv_weight, norm_gain, w_query, w_key, w_value, w_out, cotangent):
    frames, h, width, chans = video.shape
    full = n_rows * h
    own = frames * h * width
    anywhere = pl.BlockSpec(memory_space=pl.ANY)
    vmem = pl.BlockSpec(memory_space=pltpu.VMEM)
    dma = pltpu.SemaphoreType.DMA
    shape = jax.ShapeDtypeStruct(video.shape, BF)
    outs = pl.pallas_call(
        functools.partial(block, n_tm, n_rows),
        out_shape=(shape, shape),
        in_specs=[anywhere, anywhere, vmem] + [anywhere] * 5,
        out_specs=(vmem, vmem),
        scratch_shapes=[
            pltpu.VMEM((frames + 2, h + 2, width, chans), BF),
            pltpu.VMEM(conv_weight.shape, BF),
            pltpu.VMEM((chans, 3 * chans), BF),
            pltpu.VMEM((chans, chans), BF),
            pltpu.VMEM((frames, full, width, chans), BF),
            pltpu.VMEM((frames, full, width, chans), BF),
            pltpu.VMEM((own, TAPS * chans), F32),
            pltpu.VMEM((full * width, chans), BF),
            pltpu.VMEM((full * width, chans), BF),
            pltpu.VMEM((full + 2, width, chans), BF),
            pltpu.VMEM((frames, full * width, chans), BF),
            pltpu.VMEM((frames + 2, h + 2, width, chans), BF),
            dma((TAPS, TAPS)),
            dma((4,)),
            dma((2,)),
            dma((5,)),
            dma((5,)),
            dma((frames, n_rows - 1)),
            dma((frames, n_rows - 1)),
            dma((frames, n_rows - 1)),
            dma((frames, n_rows - 1)),
            dma((2,)),
            dma((2,)),
        ],
        compiler_params=pltpu.CompilerParams(
            collective_id=0, has_side_effects=True, vmem_limit_bytes=56 * 1024 * 1024
        ),
    )(
        video,
        conv_weight,
        norm_gain,
        w_query,
        w_key,
        w_value,
        w_out,
        cotangent,
    )
    return pl.pallas_call(
        settle,
        out_shape=(shape, shape),
        in_specs=[vmem] * 2,
        out_specs=(vmem, vmem),
    )(*outs)


def solution(mesh):
    n_tm, n_rows = mesh.shape["tm"], mesh.shape["rows"]
    split = P("tm", "rows", None, None)
    return jax.shard_map(
        functools.partial(local, n_tm, n_rows),
        mesh=mesh,
        in_specs=(split, P(), P(), P(), P(), P(), P(), split),
        out_specs=(split, split),
        check_vma=False,
    )
```

```python
import functools

import jax
import jax.numpy as jnp
from jax import lax
from jax.experimental import pallas as pl
from jax.experimental.pallas import tpu as pltpu
from jax.sharding import PartitionSpec as P

TAPS = 3
BF = jnp.bfloat16
F32 = jnp.float32


def mm(a, b):
    return lax.dot_general(a, b, (((1,), (0,)), ((), ())), preferred_element_type=F32)


def mm_nt(a, b):
    return lax.dot_general(a, b, (((1,), (1,)), ((), ())), preferred_element_type=F32)


def mm_tn(a, b):
    return lax.dot_general(a, b, (((0,), (0,)), ((), ())), preferred_element_type=F32)


def block(
    n_tm,
    n_rows,
    video,
    weight,
    gain,
    w_query,
    w_key,
    w_value,
    w_out,
    cot,
    block_out,
    video_grad,
    xin,
    wbuf,
    wqkv,
    wo,
    cot_full,
    conv_full,
    sums,
    act_s,
    att_s,
    gc_full,
    grad_s,
    gwin,
    w_sem,
    p_sem,
    io_sem,
    halo_send,
    halo_recv,
    cot_send,
    cot_recv,
    conv_send,
    conv_recv,
    gc_send,
    gc_recv,
):
    frames, h, width, chans = video.shape
    full = n_rows * h
    pos = full * width
    own = frames * h * width
    tm = lax.axis_index("tm")
    row = lax.axis_index("rows")
    scale = 1.0 / jnp.sqrt(jnp.float32(chans))
    first_row, last_row = row == 0, row == n_rows - 1
    has_up, has_down = row > 0, row < n_rows - 1
    has_prev, has_next = tm > 0, tm < n_tm - 1
    own_rows = pl.ds(row * h, h)

    w_copies = {
        (a, b): pltpu.make_async_copy(weight.at[a, b], wbuf.at[a, b], w_sem.at[a, b])
        for a in range(TAPS)
        for b in range(TAPS)
    }
    in_copy = pltpu.make_async_copy(video, xin.at[pl.ds(2, frames), pl.ds(1, h)], io_sem.at[0])
    cot_copy = pltpu.make_async_copy(cot, cot_full.at[:, own_rows], io_sem.at[1])
    p_copies = [
        pltpu.make_async_copy(w, wqkv.at[:, pl.ds(i * chans, chans)], p_sem.at[i])
        for i, w in enumerate((w_query, w_key, w_value))
    ] + [pltpu.make_async_copy(w_out, wo, p_sem.at[3])]

    in_copy.start()
    for a in (2, 1, 0):
        for b in range(TAPS):
            w_copies[a, b].start()
    cot_copy.start()
    for c in p_copies:
        c.start()

    barrier = pltpu.get_barrier_semaphore()

    def greet(cond, t, r):
        @pl.when(cond)
        def _():
            pl.semaphore_signal(
                barrier, inc=1, device_id=(t, r), device_id_type=pl.DeviceIdType.MESH
            )

    peers = [lax.rem(row + k, n_rows) for k in range(1, n_rows)]
    for peer in peers:
        pl.semaphore_signal(
            barrier, inc=1, device_id=(tm, peer), device_id_type=pl.DeviceIdType.MESH
        )
    greet(has_prev, tm - 1, row)
    greet(has_next, tm + 1, row)

    line = jnp.zeros((frames, width, chans), BF)

    @pl.when(first_row)
    def _():
        xin[2 : 2 + frames, 0] = line
        xin[0:2, 0] = jnp.zeros((2, width, chans), BF)

    @pl.when(last_row)
    def _():
        xin[2 : 2 + frames, h + 1] = line
        xin[0:2, h + 1] = jnp.zeros((2, width, chans), BF)

    @pl.when(tm == 0)
    def _():
        xin[0:2] = jnp.zeros((2, h + 2, width, chans), BF)

    @pl.when(tm == n_tm - 1)
    def _():
        gwin[frames : frames + 2] = jnp.zeros((2, h + 2, width, chans), BF)

    gc_full[0] = jnp.zeros((width, chans), BF)
    gc_full[full + 1] = jnp.zeros((width, chans), BF)

    wait_for = (
        (n_rows - 1)
        + jnp.where(has_prev, 1, 0)
        + jnp.where(has_next, 1, 0)
    )
    pl.semaphore_wait(barrier, wait_for)

    def remote(src, dst, send, recv, t, r):
        return pltpu.make_async_remote_copy(
            src_ref=src,
            dst_ref=dst,
            send_sem=send,
            recv_sem=recv,
            device_id=(t, r),
            device_id_type=pl.DeviceIdType.MESH,
        )

    now, before = pl.ds(2, frames), pl.ds(0, 2)
    late = pl.ds(frames - 2, 2)
    top, low = pl.ds(0, 1), pl.ds(h - 1, 1)
    halos = [
        (has_up, remote(video.at[:, top], xin.at[now, pl.ds(h + 1, 1)], halo_send.at[0], halo_recv.at[0], tm, row - 1), has_down),
        (has_down, remote(video.at[:, low], xin.at[now, pl.ds(0, 1)], halo_send.at[1], halo_recv.at[1], tm, row + 1), has_up),
        (has_next, remote(video.at[late], xin.at[before, pl.ds(1, h)], halo_send.at[2], halo_recv.at[2], tm + 1, row), has_prev),
    ]
    last = pl.ds(frames, 2)
    edges = [
        (cond, pl.ds(i, 1), halo_send.at[k], halo_recv.at[k])
        for cond, i, k in ((has_up, 0, 3), (has_down, h + 1, 4))
    ]
    passed = [
        (has_next & cond, remote(xin.at[last, i], xin.at[before, i], ss, rs, tm + 1, row), has_prev & cond)
        for cond, i, ss, rs in edges
    ]
    for cond, copy, _ in halos:
        pl.when(cond)(copy.start)

    cots = [
        remote(
            cot.at[f], cot_full.at[f, own_rows], cot_send.at[f, k], cot_recv.at[f, k], tm, peer
        )
        for f in range(frames)
        for k, peer in enumerate(peers)
    ]
    for copy in cots[: len(peers)]:
        copy.start()

    def conv_step(taps):
        lhs = jnp.concatenate(
            [xin[a : a + frames, pl.ds(b, h)].reshape(own, chans) for a, b in taps], axis=1
        )
        rhs = jnp.concatenate(
            [
                jnp.concatenate([wbuf[a, b, c] for a, b in taps], axis=0)
                for c in range(TAPS)
            ],
            axis=1,
        )
        return mm(lhs, rhs)

    near = jnp.where(first_row, 0, 2)
    far = 2 - near

    column = lax.rem(lax.broadcasted_iota(jnp.int32, (own, 1), 0), width)

    def shifted(x, by):
        rolled = pltpu.roll(x, by % own, 0)
        edge = column == (0 if by == 1 else width - 1)
        return jnp.where(edge, 0.0, rolled)

    def part(c):
        return sums[:, c * chans : (c + 1) * chans]

    in_copy.wait()
    for b in range(TAPS):
        w_copies[2, b].wait()
    pl.when(has_down & has_up)(halos[0][1].wait_recv)
    sums[...] = conv_step([(2, 1), (2, near)])
    pl.when(has_down & first_row)(halos[0][1].wait_recv)
    pl.when(has_up)(halos[1][1].wait_recv)
    for cond, copy, _ in passed:
        pl.when(cond)(copy.start)
    for copy in cots[len(peers) :]:
        copy.start()
    for a in (1, 0):
        for b in range(TAPS):
            w_copies[a, b].wait()
    pl.when(has_prev)(halos[2][1].wait_recv)
    pl.when(has_prev & has_down & has_up)(passed[1][1].wait_recv)
    sums[...] += conv_step([(1, 1), (1, near), (0, 1), (0, near)])
    pl.when(has_prev & has_down & first_row)(passed[1][1].wait_recv)
    pl.when(has_prev & has_up)(passed[0][1].wait_recv)
    sums[...] += conv_step([(2, far), (1, far), (0, far)])
    conv = (shifted(part(0), 1) + part(1) + shifted(part(2), -1)).astype(BF)
    conv_full[:, own_rows] = conv.reshape(frames, h, width, chans)
    convs = [
        [
            remote(
                conv_full.at[f, own_rows],
                conv_full.at[f, own_rows],
                conv_send.at[f, k],
                conv_recv.at[f, k],
                tm,
                peer,
            )
            for k, peer in enumerate(peers)
        ]
        for f in range(frames)
    ]
    for group in convs:
        for copy in group:
            copy.start()
    for c in p_copies:
        c.wait()
    cot_copy.wait()
    g = gain[...].reshape(1, chans)
    mine = pl.ds(pl.multiple_of(row * (h * width), h * width), h * width)
    backs = []
    for f in range(frames):
        for copy in cots[f * len(peers) : (f + 1) * len(peers)]:
            copy.wait_recv()
        grad_s[f] = mm_nt(cot_full[f].reshape(pos, chans), wo[...]).astype(BF)
        for copy in convs[f]:
            copy.wait_recv()
        convf = conv_full[f].reshape(pos, chans).astype(F32)
        inverse = lax.rsqrt(jnp.mean(convf * convf, axis=-1, keepdims=True) + 1e-06)
        normed = convf * inverse * g
        sigma = 1.0 / (1.0 + jnp.exp(-normed))
        act = (normed * sigma).astype(BF)
        act_s[...] = act
        qkv = mm(act, wqkv[...]).astype(BF)
        query = qkv[:, :chans]
        key = qkv[:, chans : 2 * chans]
        value = qkv[:, 2 * chans :]
        cot_f = cot_full[f].reshape(pos, chans)
        grad_att = grad_s[f]
        scores = mm_nt(query, key) * scale
        peak = jnp.max(scores, axis=-1, keepdims=True)
        expo = jnp.exp(scores - peak)
        probs = expo / jnp.sum(expo, axis=-1, keepdims=True)
        probs_b = probs.astype(BF)
        attended = mm(probs_b, value).astype(BF)
        att_s[...] = attended
        delta = jnp.sum(grad_att.astype(F32) * attended.astype(F32), axis=-1, keepdims=True)
        dprob = mm_nt(grad_att, value)
        dscore = (probs * (dprob - delta)).astype(BF)
        grad_q = (mm(dscore, key) * scale).astype(BF)
        grad_k = (mm_tn(dscore, query) * scale).astype(BF)
        grad_v = mm_tn(probs_b, grad_att).astype(BF)
        grads = jnp.concatenate([grad_q, grad_k, grad_v], axis=1)
        grad_act = cot_f.astype(F32) + mm_nt(grads, wqkv[...])
        scaled = grad_act * sigma * (1.0 + normed * (1.0 - sigma)) * g
        grad_conv = inverse * (
            scaled
            - convf * inverse * inverse * jnp.mean(scaled * convf, axis=-1, keepdims=True)
        )
        gc_full[1 : full + 1] = grad_conv.astype(BF).reshape(full, width, chans)
        gwin[f] = gc_full[pl.ds(row * h, h + 2)]
        if f < 2:
            back = remote(
                gwin.at[f], gwin.at[frames + f], gc_send.at[f], gc_recv.at[f], tm - 1, row
            )
            pl.when(has_prev)(back.start)
            backs.append(back)
        projected = mm(att_s[mine], wo[...])
        out = (act_s[mine].astype(F32) + projected).astype(BF)
        block_out[f] = out.reshape(h, width, chans)

    def back_step(a):
        lhs = jnp.concatenate(
            [
                gwin[2 - a : 2 - a + frames, 2 - b : 2 - b + h].reshape(own, chans)
                for b in range(TAPS)
            ],
            axis=1,
        )
        rhs = jnp.concatenate(
            [wbuf[a, b].reshape(TAPS * chans, chans) for b in range(TAPS)], axis=1
        )
        return mm_nt(lhs, rhs)

    sums[...] = back_step(2)
    pl.when(has_next)(backs[0].wait_recv)
    sums[...] += back_step(1)
    pl.when(has_next)(backs[1].wait_recv)
    sums[...] += back_step(0)
    result = shifted(part(0), -1) + part(1) + shifted(part(2), 1)
    video_grad[...] = result.astype(BF).reshape(frames, h, width, chans)

    for cond, copy, _ in halos + passed:
        pl.when(cond)(copy.wait_send)
    for copy in sum(convs, cots):
        copy.wait_send()
    for back in backs:
        pl.when(has_prev)(back.wait_send)


def settle(a, b, a_out, b_out):
    a_out[...] = a[...]
    b_out[...] = b[...]


def local(n_tm, n_rows, video, conv_weight, norm_gain, w_query, w_key, w_value, w_out, cotangent):
    frames, h, width, chans = video.shape
    full = n_rows * h
    own = frames * h * width
    anywhere = pl.BlockSpec(memory_space=pl.ANY)
    vmem = pl.BlockSpec(memory_space=pltpu.VMEM)
    dma = pltpu.SemaphoreType.DMA
    shape = jax.ShapeDtypeStruct(video.shape, BF)
    outs = pl.pallas_call(
        functools.partial(block, n_tm, n_rows),
        out_shape=(shape, shape),
        in_specs=[anywhere, anywhere, vmem] + [anywhere] * 5,
        out_specs=(vmem, vmem),
        scratch_shapes=[
            pltpu.VMEM((frames + 2, h + 2, width, chans), BF),
            pltpu.VMEM(conv_weight.shape, BF),
            pltpu.VMEM((chans, 3 * chans), BF),
            pltpu.VMEM((chans, chans), BF),
            pltpu.VMEM((frames, full, width, chans), BF),
            pltpu.VMEM((frames, full, width, chans), BF),
            pltpu.VMEM((own, TAPS * chans), F32),
            pltpu.VMEM((full * width, chans), BF),
            pltpu.VMEM((full * width, chans), BF),
            pltpu.VMEM((full + 2, width, chans), BF),
            pltpu.VMEM((frames, full * width, chans), BF),
            pltpu.VMEM((frames + 2, h + 2, width, chans), BF),
            dma((TAPS, TAPS)),
            dma((4,)),
            dma((2,)),
            dma((5,)),
            dma((5,)),
            dma((frames, n_rows - 1)),
            dma((frames, n_rows - 1)),
            dma((frames, n_rows - 1)),
            dma((frames, n_rows - 1)),
            dma((2,)),
            dma((2,)),
        ],
        compiler_params=pltpu.CompilerParams(
            collective_id=0, has_side_effects=True, vmem_limit_bytes=56 * 1024 * 1024
        ),
    )(
        video,
        conv_weight,
        norm_gain,
        w_query,
        w_key,
        w_value,
        w_out,
        cotangent,
    )
    return pl.pallas_call(
        settle,
        out_shape=(shape, shape),
        in_specs=[vmem] * 2,
        out_specs=(vmem, vmem),
    )(*outs)


def solution(mesh):
    n_tm, n_rows = mesh.shape["tm"], mesh.shape["rows"]
    split = P("tm", "rows", None, None)
    return jax.shard_map(
        functools.partial(local, n_tm, n_rows),
        mesh=mesh,
        in_specs=(split, P(), P(), P(), P(), P(), P(), split),
        out_specs=(split, split),
        check_vma=False,
    )
```
